32 devices in a mesh: segment: 4 (over y, core), row: 2 (over x), dp: 4 (over z).
Axes of the slice: x: 2, y: 2, z: 4, core: 2. Of those that a mesh axis runs over, the one named last changes fastest.
Arguments:
- fresh: float32 [2, 4, 16, 16, 256], P(None, 'dp', 'row'), may hold values from -6 to 6
- target: float32 [1, 4, 16, 16, 256], P(None, 'dp', 'row'), may hold values from -6 to 6
- carried: float32 [4, 4, 16, 16, 256], P('segment', 'dp', 'row'), may hold values from -6 to 6
- returning: float32 [4, 2, 4, 16, 16, 256], P('segment', None, 'dp', 'row'), may hold values from -6 to 6
- weights: float32 [4, 2, 2, 1152, 128], P('segment'), may hold values from -0.09375 to 0.09375
- section_blocks: int32 [4], P('segment'), may hold values from 1 to 2, as said below
Outputs:
- grad_weights: float32 [4, 2, 2, 1152, 128], P('segment', None, None, ('row', 'dp'))
- leaving: float32 [4, 4, 16, 16, 256], P('segment', 'dp', 'row')
- sent_back: float32 [4, 2, 4, 16, 16, 256], P('segment', None, 'dp', 'row')
The draws below stay inside these ranges and needn't reach their ends.
Inputs may be any that keep to these rules, and one draw needn't show every extreme that they name: `section_blocks`: each section holds one or two blocks; some section holds two and some one.
All inputs are finite; a program needn't handle non-finite values.
Results may differ from the reference program's by a relative error of at most 0.00012.
Values sent between devices are 32-bit elements; how exact they have to be, the bound alone decides.
A program may use at most 64 MiB of HBM per device.

```python
import math
import jax
import jax.numpy as jnp
from jax import lax

C = 128
BLK = 2
TICKS = 2
WD = 16
BATCH = 4
HEIGHT = 16
N_SEGMENT = 4


def draw_section_blocks(key, part):
    first_key, second_key = jax.random.split(jax.random.fold_in(key, 7))
    counts = 1 + jax.random.randint(first_key, (N_SEGMENT,), 0, 2)
    ordering = jax.random.permutation(second_key, N_SEGMENT)
    counts = counts.at[ordering[0]].set(2).at[ordering[1]].set(1)
    return counts.astype(jnp.int32)


def levels(key, dims, pieces, least, top_value):
    factor_of = 1.0
    for position, shards_of in pieces:
        heights = jax.random.uniform(jax.random.fold_in(jax.random.fold_in(key, 6), position), (shards_of,), jnp.float32, least / len(pieces), top_value / len(pieces))
        factor_of = factor_of * jnp.repeat(jnp.exp(heights), dims[position] // shards_of).reshape((-1,) + (1,) * (len(dims) - 1 - position))
    return factor_of


def gaussian(key, shape, width, bound, cuts=(), kind=jnp.bfloat16):
    result = jax.random.normal(key, shape, jnp.float32) * width
    if len(cuts) > 0:
        result = levels(key, shape, cuts, -0.22, 0.18) * result
    return jnp.clip(result, min=-bound, max=bound).astype(kind)


def setup_inputs(seed: int = 0) -> dict:
    keys = jax.random.split(jax.random.key(seed), 7)
    fresh = gaussian(keys[0], (TICKS, BATCH, HEIGHT, WD, 2 * C), 1.0, 6.0, ((1, 4), (2, 2)), jnp.float32)
    target = gaussian(keys[1], (TICKS - 1, BATCH, HEIGHT, WD, 2 * C), 1.0, 6.0, ((1, 4), (2, 2)), jnp.float32)
    carried = gaussian(keys[2], (N_SEGMENT, BATCH, HEIGHT, WD, 2 * C), 1.0, 6.0, ((0, 4), (1, 4), (2, 2)), jnp.float32)
    returning = gaussian(keys[3], (N_SEGMENT, 2, BATCH, HEIGHT, WD, 2 * C), 1.0, 6.0, ((0, 4), (2, 4), (3, 2)), jnp.float32)
    weights = gaussian(keys[4], (N_SEGMENT, BLK, 2, 9 * C, C), (36 * C) ** -0.5, 0.09375, ((0, 4),), jnp.float32)
    section_blocks = draw_section_blocks(jax.random.fold_in(keys[6], 71), 0)
    return dict(fresh=fresh, target=target, carried=carried, returning=returning, weights=weights, section_blocks=section_blocks)


HIGHEST = lax.Precision.HIGHEST

def convolve(source, kernel):
    chans = kernel.shape[1]
    return lax.conv_general_dilated(source, kernel.reshape(3, 3, chans, chans), (1, 1), 'SAME', dimension_numbers=('NHWC', 'HWIO', 'NHWC'), precision=HIGHEST)

def branch(source, kernel):
    return convolve(jax.nn.silu(source), kernel)

def forward_block(state, first_kernel, second_kernel):
    chans = first_kernel.shape[1]
    upper_half = state[..., :chans] + branch(state[..., chans:], first_kernel)
    lower_half = state[..., chans:] + branch(upper_half, second_kernel)
    return jnp.concatenate([upper_half, lower_half], axis=-1)

def backward_block(outputs, grads, first_kernel, second_kernel):
    chans = first_kernel.shape[1]
    upper_half, lower_half = (outputs[..., :chans], outputs[..., chans:])
    grad_upper, grad_lower = (grads[..., :chans], grads[..., chans:])
    rebuilt, pull_second = jax.vjp(branch, upper_half, second_kernel)
    lower_in = lower_half - rebuilt
    added_grad, grad_second = pull_second(grad_lower)
    grad_upper = grad_upper + added_grad
    rebuilt, pull_first = jax.vjp(branch, lower_in, first_kernel)
    upper_in = upper_half - rebuilt
    added_grad, grad_first = pull_first(grad_upper)
    grad_lower = grad_lower + added_grad
    return (jnp.concatenate([upper_in, lower_in], axis=-1), jnp.concatenate([grad_upper, grad_lower], axis=-1), grad_first, grad_second)

def reference(fresh, target, carried, returning, weights, section_blocks):
    inputs = [carried[segment_id] for segment_id in range(N_SEGMENT)]
    pairs = [(returning[segment_id, 0], returning[segment_id, 1]) for segment_id in range(N_SEGMENT)]
    running = [jnp.zeros((BLK, 2, 9 * C, C), jnp.float32) for segment_id in range(N_SEGMENT)]
    produced = []
    sent = []
    for window_tick in range(TICKS):
        produced = []
        sent = []
        for segment_id in range(N_SEGMENT):
            doubled = section_blocks[segment_id] == 2
            factor = doubled.astype(jnp.float32)
            source = fresh[window_tick] if segment_id == 0 else inputs[segment_id]
            once = forward_block(source, weights[segment_id, 0, 0], weights[segment_id, 0, 1])
            twice = forward_block(once, weights[segment_id, 1, 0], weights[segment_id, 1, 1])
            produced.append(jnp.where(doubled, twice, once))
            outputs, grads = pairs[segment_id]
            back_in, back_grad, first_one, second_one = backward_block(outputs, grads, weights[segment_id, 1, 0], weights[segment_id, 1, 1])
            outputs = jnp.where(doubled, back_in, outputs)
            grads = jnp.where(doubled, back_grad, grads)
            back_in, back_grad, first_zero, second_zero = backward_block(outputs, grads, weights[segment_id, 0, 0], weights[segment_id, 0, 1])
            tick_grads = jnp.stack([jnp.stack([first_zero, second_zero]), jnp.stack([first_one, second_one]) * factor])
            running[segment_id] = running[segment_id] + tick_grads
            sent.append((back_in, back_grad))
        if window_tick < TICKS - 1:
            inputs = [produced[0]] + produced[:-1]
            last_out = produced[-1]
            pairs = sent[1:] + [(last_out, last_out - target[window_tick])]
    grad_weights = jnp.stack(running) / math.sqrt(TICKS * BATCH * HEIGHT * WD)
    leaving = jnp.stack(produced)
    sent_back = jnp.stack([jnp.stack([pair_in, pair_grad]) for pair_in, pair_grad in sent])
    return (grad_weights, leaving, sent_back)
```

```python
import functools
import math

import jax
import jax.numpy as jnp
from jax import lax
from jax.experimental import pallas as pl
from jax.experimental.pallas import tpu as pltpu
from jax.sharding import PartitionSpec as P

MESH = pl.DeviceIdType.MESH
SRC, OUT, GRAD = 0, 1, 2


def split_float(value):
    high = value.astype(jnp.bfloat16)
    low = (value - high.astype(jnp.float32)).astype(jnp.bfloat16)
    return high, low


def kernel_body(
    sizes,
    fresh,
    target,
    carried,
    returning,
    weights,
    blocks,
    grads_out,
    leaving,
    sent_back,
    st,
    produced,
    aims,
    keep,
    w_fwd,
    w_flip,
    pad_fwd,
    pad_src,
    pad_cot,
    src_t,
    sums,
    landed,
    row_send,
    row_recv,
    late_send,
    late_recv,
    seg_send,
    seg_recv,
    red_send,
    red_recv,
):
    ticks, seg_n, row_n, dp_n, width, local, chans, taps, reach, scale = sizes
    cells = local * row_n
    levels = dp_n.bit_length() - 1
    chunk = (9 * chans) // (row_n * dp_n)
    seg = lax.axis_index("segment")
    row = lax.axis_index("row")
    dp = lax.axis_index("dp")
    not_first = seg > 0
    not_last = seg < seg_n - 1

    barrier = pltpu.get_barrier_semaphore()
    row_peers = [lax.rem(row + k, row_n) for k in range(1, row_n)]
    dp_peers = [
        dp + (1 << lev) - 2 * (1 << lev) * lax.rem(dp // (1 << lev), 2) for lev in range(levels)
    ]
    for peer in row_peers:
        pl.semaphore_signal(barrier, inc=1, device_id={"row": peer}, device_id_type=MESH)
    for peer in dp_peers:
        pl.semaphore_signal(barrier, inc=1, device_id={"dp": peer}, device_id_type=MESH)

    @pl.when(not_first)
    def _():
        pl.semaphore_signal(barrier, inc=1, device_id={"segment": seg - 1}, device_id_type=MESH)

    @pl.when(not_last)
    def _():
        pl.semaphore_signal(barrier, inc=1, device_id={"segment": seg + 1}, device_id_type=MESH)

    always = len(row_peers) + len(dp_peers)
    pl.semaphore_wait(barrier, always + not_first.astype(jnp.int32) + not_last.astype(jnp.int32))

    mine = pl.ds(pl.multiple_of(row * local, local), local)

    def lanes(half):
        return slice(half * chans, (half + 1) * chans)

    order = [(SRC, 1), (OUT, 0), (GRAD, 1), (SRC, 0), (OUT, 1), (GRAD, 0)]

    def row_copy(place, k, ref, send, recv):
        return pltpu.make_async_remote_copy(
            src_ref=ref,
            dst_ref=ref,
            send_sem=send.at[place, k],
            recv_sem=recv.at[place, k],
            device_id={"row": row_peers[k]},
            device_id_type=MESH,
        )

    def gathers(place):
        field, half = order[place]
        return [
            row_copy(place, k, st.at[0, field, half, mine], row_send, row_recv)
            for k in range(row_n - 1)
        ]

    for place, (field, half) in enumerate(order):
        if field == SRC:
            first = jnp.full((local, chans), seg, jnp.int32) == 0
            value = jnp.where(first, fresh[0, :, lanes(half)], carried[:, lanes(half)])
        else:
            value = returning[field - 1, :, lanes(half)]
        st[0, field, half, mine] = value
        for copy in gathers(place):
            copy.start()

    def fresh_copies():
        return [
            row_copy(2 * tick + half - 2, k, st.at[tick, SRC, half, mine], late_send, late_recv)
            for tick in range(1, ticks)
            for half in range(2)
            for k in range(row_n - 1)
        ]

    def target_copies():
        return [
            row_copy(2 * tick + half, k, aims.at[tick, half, mine], late_send, late_recv)
            for tick in range(ticks - 1)
            for half in range(2)
            for k in range(row_n - 1)
        ]

    @pl.when(seg == 0)
    def _():
        for tick in range(1, ticks):
            for half in range(2):
                st[tick, SRC, half, mine] = fresh[tick, :, lanes(half)]
        for copy in fresh_copies():
            copy.start()

    @pl.when(seg == seg_n - 1)
    def _():
        for tick in range(ticks - 1):
            for half in range(2):
                aims[tick, half, mine] = target[tick, :, lanes(half)]
        for copy in target_copies():
            copy.start()

    def store_kernel(ref, pair, tap, value):
        high, low = split_float(value)
        base = tap * (2 * chans)
        for part in range(2):
            rows = pl.ds(pl.multiple_of(base + part * chans, chans), chans)
            ref[pair, rows, :chans] = high
            ref[pair, rows, chans:] = low

    def prepare(index, carry):
        pair = index // 9
        tap = index - 9 * pair
        value = weights[pair, pl.ds(pl.multiple_of(tap * chans, chans), chans), :]
        store_kernel(w_fwd, pair, tap, value)
        store_kernel(w_flip, pair, 8 - tap, value.T)
        return carry

    lax.fori_loop(0, 36, prepare, 0)

    rim = jnp.zeros((width, 2 * chans), jnp.bfloat16)
    for side in range(3):
        for start in (0, width + cells):
            pad_fwd[side, start : start + width] = rim
            pad_src[side, start : start + width] = rim
            for slot in range(4):
                pad_cot[slot, side, start : start + width] = rim

    column = lax.rem(lax.broadcasted_iota(jnp.int32, (cells, chans), 0), width)

    def fill(view, value):
        before = jnp.where(column == 0, 0.0, pltpu.roll(value, 1, 0))
        after = jnp.where(column == width - 1, 0.0, pltpu.roll(value, cells - 1, 0))
        for side, shifted in enumerate((before, value, after)):
            high, low = split_float(shifted)
            view[side, width : width + cells, :chans] = high
            view[side, width : width + cells, chans:] = low

    def conv(view, kernel):
        patches = jnp.concatenate(
            [
                view[tap % 3, (tap // 3) * width : (tap // 3) * width + cells, :]
                for tap in range(9)
            ],
            axis=1,
        )
        both = jnp.dot(patches, kernel, preferred_element_type=jnp.float32)
        return both[:, :chans] + both[:, chans:]

    doubled = jnp.full((cells, chans), blocks[0], jnp.int32) == 2

    def pair_of(step):
        return 2 * (1 - step // 2) + 1 - step % 2

    def forward_step(tick, step):
        even = step % 2 == 0
        source, goal = (1, 0) if even else (0, 1)
        held = st if step < 2 else keep
        if step == 0:
            value = st[tick, SRC, source]
        elif step == 1:
            value = keep[source]
        else:
            value = keep[source]
        fill(pad_fwd, jax.nn.silu(value))
        base = st[tick, SRC, goal] if step < 2 else keep[goal]
        fresh_value = base + conv(pad_fwd, w_fwd[step])
        if step < 2:
            keep[goal] = fresh_value
        else:
            chosen = jnp.where(doubled, fresh_value, keep[goal])
            keep[goal] = fresh_value
            produced[tick, SRC, goal] = chosen

    def backward_open(tick, step):
        even = step % 2 == 0
        held = (lambda f, h: st[tick, f, h]) if step == 0 else (lambda f, h: produced[tick, f, h])
        if step == 0:
            source, cot = st[tick, OUT, 0], st[tick, GRAD, 1]
        elif even:
            source, cot = produced[tick, OUT, 0], produced[tick, GRAD, 1]
        else:
            source, cot = produced[tick, OUT, 1], produced[tick, GRAD, 0]
        if step == 1:
            source, cot = produced[tick, OUT, 1], produced[tick, GRAD, 0]
        logistic = jax.nn.sigmoid(source)
        active = source * logistic
        fill(pad_src, active)
        fill(pad_cot.at[step], cot)
        high, low = split_float(active.T)
        src_t[step, :chans] = high
        src_t[step, chans:] = low
        return logistic * (1.0 + source * (1.0 - logistic))

    def backward_close(tick, step, slope):
        even = step % 2 == 0
        out_goal, grad_goal = (1, 0) if even else (0, 1)
        holder = st if step < 2 else produced
        out_old = holder[tick, OUT, out_goal]
        grad_old = holder[tick, GRAD, grad_goal]
        rebuilt = conv(pad_src, w_fwd[pair_of(step)])
        added = conv(pad_cot.at[step], w_flip[pair_of(step)]) * slope
        out_new = out_old - rebuilt
        grad_new = grad_old + added
        produced[tick, OUT, out_goal] = out_new
        produced[tick, GRAD, grad_goal] = grad_new
        if step == 1:
            for half in range(2):
                for field in (OUT, GRAD):
                    produced[tick, field, half] = jnp.where(
                        doubled, produced[tick, field, half], st[tick, field, half]
                    )

    first_tap = jnp.minimum((row * (9 * chans // row_n)) // chans, 9 - taps)

    def kernel_grads(tick, step):
        pair = pair_of(step)
        for extra in range(taps):
            other = 8 - first_tap - extra
            down = other // 3
            side = other - 3 * down
            cots = pad_cot[step, side, pl.ds(pl.multiple_of(down * width, width), cells), :]
            four = jnp.dot(src_t[step], cots, preferred_element_type=jnp.float32)
            two = four[:chans] + four[chans:]
            value = two[:, :chans] + two[:, chans:]
            rows = slice(extra * chans, (extra + 1) * chans)
            if tick > 0:
                value = value + sums[pair, rows]
            sums[pair, rows] = value

    def seg_copy(tick, field, half):
        by = 1 if field == SRC else -1
        slot = (tick * 3 + field) * 2 + half

        def make(to):
            return pltpu.make_async_remote_copy(
                src_ref=produced.at[tick, field, half],
                dst_ref=st.at[tick + 1, field, half],
                send_sem=seg_send.at[slot],
                recv_sem=seg_recv.at[slot],
                device_id={"segment": to},
                device_id_type=MESH,
            )

        return make, by

    def seg_start(tick, field, half):
        make, by = seg_copy(tick, field, half)

        @pl.when(not_last if by > 0 else not_first)
        def _():
            make(seg + by).start()

    def seg_wait_recv(tick, field, half):
        make, by = seg_copy(tick, field, half)

        @pl.when(not_first if by > 0 else not_last)
        def _():
            make(seg - by).wait_recv()

    def seg_wait_send(tick, field, half):
        make, by = seg_copy(tick, field, half)

        @pl.when(not_last if by > 0 else not_first)
        def _():
            make(seg + by).wait_send()

    offset = row * (9 * chans // row_n) - first_tap * chans

    def chunk_rows(index):
        return pl.ds(pl.multiple_of(offset + index * chunk, 16), chunk)

    def red_places(level):
        span = 1 << (level + 1)
        count = dp_n // span
        start = sum(dp_n >> (lev + 1) for lev in range(level))
        return span, count, start

    def red_copies(pair, level):
        span, count, start = red_places(level)
        away = lax.rem(dp_peers[level], span)
        return [
            pltpu.make_async_remote_copy(
                src_ref=sums.at[pair, chunk_rows(away + span * j)],
                dst_ref=landed.at[pair, start + j],
                send_sem=red_send.at[pair, start + j],
                recv_sem=red_recv.at[pair, start + j],
                device_id={"dp": dp_peers[level]},
                device_id_type=MESH,
            )
            for j in range(count)
        ]

    def red_start(pair, level):
        if level < levels:
            for copy in red_copies(pair, level):
                copy.start()

    def red_finish(pair, level):
        span, count, start = red_places(level)
        own = lax.rem(dp, span)
        for j, copy in enumerate(red_copies(pair, level)):
            copy.wait_recv()
            rows = chunk_rows(own + span * j)
            sums[pair, rows] = sums[pair, rows] + landed[pair, start + j]

    for tick in range(ticks):
        final = tick == ticks - 1
        for step in range(4):
            if tick == 0:
                if step == 0:
                    for place in range(3):
                        for copy in gathers(place):
                            copy.wait_recv()
            elif step == 0:
                seg_wait_recv(tick - 1, OUT, 0)
                seg_wait_recv(tick - 1, GRAD, 1)
            slope = backward_open(tick, step)
            if final:
                kernel_grads(tick, step)
                red_start(pair_of(step), 0)
            if step == 0:
                if tick == 0:
                    for place in range(3, 6):
                        for copy in gathers(place):
                            copy.wait_recv()
                else:
                    seg_wait_recv(tick - 1, OUT, 1)
                    seg_wait_recv(tick - 1, GRAD, 0)
            if not final:
                if step == 0 and tick > 0:
                    seg_wait_recv(tick - 1, SRC, 0)
                    seg_wait_recv(tick - 1, SRC, 1)
                forward_step(tick, step)
            backward_close(tick, step, slope)
            if not final and step >= 2:
                even = step % 2 == 0
                seg_start(tick, SRC, 0 if even else 1)
                seg_start(tick, OUT, 1 if even else 0)
                seg_start(tick, GRAD, 0 if even else 1)
        if not final:
            if tick == 0:

                @pl.when(seg == 0)
                def _():
                    for copy in fresh_copies():
                        copy.wait_recv()

                @pl.when(seg == seg_n - 1)
                def _():
                    for copy in target_copies():
                        copy.wait_recv()

            @pl.when(seg == seg_n - 1)
            def _(tick=tick):
                for half in range(2):
                    value = produced[tick, SRC, half]
                    st[tick + 1, OUT, half] = value
                    st[tick + 1, GRAD, half] = value - aims[tick, half]

            for step in range(4):
                kernel_grads(tick, step)
        else:
            if tick > 0:
                seg_wait_recv(tick - 1, SRC, 0)
                seg_wait_recv(tick - 1, SRC, 1)
            for step in range(4):
                if levels > 0:
                    red_finish(pair_of(step), 0)
                    red_start(pair_of(step), 1)
                forward_step(tick, step)

    last = ticks - 1
    for half in range(2):
        leaving[:, lanes(half)] = produced[last, SRC, half, mine]
        for field in (OUT, GRAD):
            sent_back[field - 1, :, lanes(half)] = produced[last, field, half, mine]

    for level in range(1, levels):
        for step in range(4):
            red_finish(pair_of(step), level)
            red_start(pair_of(step), level + 1)
    twice = jnp.full((chunk, chans), blocks[0], jnp.int32) == 2
    for pair in range(4):
        total = sums[pair, chunk_rows(dp)] * scale
        if pair >= 2:
            total = jnp.where(twice, total, 0.0)
        grads_out[pair] = total

    for place in range(6):
        for copy in gathers(place):
            copy.wait_send()

    @pl.when(seg == 0)
    def _():
        for copy in fresh_copies():
            copy.wait_send()

    @pl.when(seg == seg_n - 1)
    def _():
        for copy in target_copies():
            copy.wait_send()

    for tick in range(ticks - 1):
        for field in (SRC, OUT, GRAD):
            for half in range(2):
                seg_wait_send(tick, field, half)
    for level in range(levels):
        for pair in range(4):
            for copy in red_copies(pair, level):
                copy.wait_send()


def per_device(axis_sizes, fresh, target, carried, returning, weights, section_blocks):
    seg_n, row_n, dp_n = axis_sizes
    ticks, crops, rows_here, width, both = fresh.shape
    assert crops == 1 and dp_n & (dp_n - 1) == 0
    chans = both // 2
    local = rows_here * width
    cells = local * row_n
    held = 9 * chans // row_n
    taps = max(-(-(r + 1) * held // chans) - r * held // chans for r in range(row_n))
    reach = dp_n - 1
    chunk = held // dp_n
    scale = 1.0 / math.sqrt(ticks * dp_n * cells)
    sizes = (ticks, seg_n, row_n, dp_n, width, local, chans, taps, reach, scale)
    pairs = 4
    f32, b16 = jnp.float32, jnp.bfloat16
    padded = cells + 2 * width
    dma = pltpu.SemaphoreType.DMA
    peers = max(row_n - 1, 1)
    late = 2 * max(ticks - 1, 1)
    vmem = pl.BlockSpec(memory_space=pltpu.VMEM)
    flops = ticks * 4 * (3 * 9 + taps) * 2 * cells * chans * chans * 4
    grads_out, leaving, sent_back = pl.pallas_call(
        functools.partial(kernel_body, sizes),
        out_shape=(
            jax.ShapeDtypeStruct((pairs, chunk, chans), f32),
            jax.ShapeDtypeStruct((local, both), f32),
            jax.ShapeDtypeStruct((2, local, both), f32),
        ),
        in_specs=[vmem] * 5 + [pl.BlockSpec(memory_space=pltpu.SMEM)],
        out_specs=(vmem, vmem, vmem),
        scratch_shapes=[
            pltpu.VMEM((ticks, 3, 2, cells, chans), f32),
            pltpu.VMEM((ticks, 3, 2, cells, chans), f32),
            pltpu.VMEM((max(ticks - 1, 1), 2, cells, chans), f32),
            pltpu.VMEM((2, cells, chans), f32),
            pltpu.VMEM((pairs, 18 * chans, 2 * chans), b16),
            pltpu.VMEM((pairs, 18 * chans, 2 * chans), b16),
            pltpu.VMEM((3, padded, 2 * chans), b16),
            pltpu.VMEM((3, padded, 2 * chans), b16),
            pltpu.VMEM((4, 3, padded, 2 * chans), b16),
            pltpu.VMEM((4, 2 * chans, cells), b16),
            pltpu.VMEM((pairs, taps * chans, chans), f32),
            pltpu.VMEM((pairs, max(reach, 1), chunk, chans), f32),
            dma((6, peers)),
            dma((6, peers)),
            dma((late, peers)),
            dma((late, peers)),
            dma((6 * ticks,)),
            dma((6 * ticks,)),
            dma((pairs, max(reach, 1))),
            dma((pairs, max(reach, 1))),
        ],
        cost_estimate=pl.CostEstimate(flops=flops, bytes_accessed=1 << 22, transcendentals=1 << 20),
        compiler_params=pltpu.CompilerParams(
            collective_id=0, has_side_effects=True, vmem_limit_bytes=48 << 20
        ),
    )(
        fresh.reshape(ticks, local, both),
        target.reshape(-1, local, both),
        carried.reshape(local, both),
        returning.reshape(2, local, both),
        weights.reshape(pairs, 9 * chans, chans),
        section_blocks,
    )
    return (
        grads_out.reshape(1, 2, 2, chunk, chans),
        leaving.reshape(1, 1, rows_here, width, both),
        sent_back.reshape(1, 2, 1, rows_here, width, both),
    )


def solution(mesh):
    axis_sizes = (mesh.shape["segment"], mesh.shape["row"], mesh.shape["dp"])
    return jax.shard_map(
        functools.partial(per_device, axis_sizes),
        mesh=mesh,
        in_specs=(
            P(None, "dp", "row", None, None),
            P(None, "dp", "row", None, None),
            P("segment", "dp", "row", None, None),
            P("segment", None, "dp", "row", None, None),
            P("segment", None, None, None, None),
            P("segment"),
        ),
        out_specs=(
            P("segment", None, None, ("row", "dp"), None),
            P("segment", "dp", "row", None, None),
            P("segment", None, "dp", "row", None, None),
        ),
        check_vma=False,
    )
```

```python
import functools
import math

import jax
import jax.numpy as jnp
from jax import lax
from jax.experimental import pallas as pl
from jax.experimental.pallas import tpu as pltpu
from jax.sharding import PartitionSpec as P

MESH = pl.DeviceIdType.MESH
SRC, OUT, GRAD = 0, 1, 2


def split_float(value):
    high = value.astype(jnp.bfloat16)
    low = (value - high.astype(jnp.float32)).astype(jnp.bfloat16)
    return high, low


def kernel_body(
    sizes,
    fresh,
    target,
    carried,
    returning,
    weights,
    blocks,
    grads_out,
    leaving,
    sent_back,
    st,
    produced,
    aims,
    keep,
    w_fwd,
    w_flip,
    pad_fwd,
    pad_src,
    pad_cot,
    src_t,
    sums,
    landed,
    row_send,
    row_recv,
    late_send,
    late_recv,
    seg_send,
    seg_recv,
    red_send,
    red_recv,
    held_weights,
    own_sem,
    late_sem,
    weight_sem,
):
    ticks, seg_n, row_n, dp_n, width, local, chans, taps, reach, scale = sizes
    cells = local * row_n
    levels = dp_n.bit_length() - 1
    chunk = (9 * chans) // (row_n * dp_n)
    seg = lax.axis_index("segment")
    row = lax.axis_index("row")
    dp = lax.axis_index("dp")
    not_first = seg > 0
    not_last = seg < seg_n - 1

    barrier = pltpu.get_barrier_semaphore()
    row_peers = [lax.rem(row + k, row_n) for k in range(1, row_n)]
    dp_peers = [
        dp + (1 << lev) - 2 * (1 << lev) * lax.rem(dp // (1 << lev), 2) for lev in range(levels)
    ]
    for peer in row_peers:
        pl.semaphore_signal(barrier, inc=1, device_id={"row": peer}, device_id_type=MESH)
    for peer in dp_peers:
        pl.semaphore_signal(barrier, inc=1, device_id={"dp": peer}, device_id_type=MESH)

    @pl.when(not_first)
    def _():
        pl.semaphore_signal(barrier, inc=1, device_id={"segment": seg - 1}, device_id_type=MESH)

    @pl.when(not_last)
    def _():
        pl.semaphore_signal(barrier, inc=1, device_id={"segment": seg + 1}, device_id_type=MESH)

    mine = pl.ds(pl.multiple_of(row * local, local), local)

    def lanes(half):
        return slice(half * chans, (half + 1) * chans)

    order = [(OUT, 0), (GRAD, 1), (OUT, 1), (GRAD, 0), (SRC, 1), (SRC, 0)]

    def fresh_part(place):
        field, half = order[place]
        return fresh.at[0, :, lanes(half)]

    def plain_part(place):
        field, half = order[place]
        if field == SRC:
            return carried.at[:, lanes(half)]
        return returning.at[field - 1, :, lanes(half)]

    def own_copy(place, part):
        field, half = order[place]
        return pltpu.make_async_copy(part, st.at[0, field, half, mine], own_sem.at[place])

    def row_copies(place, part, goal, send, recv):
        return [
            pltpu.make_async_remote_copy(
                src_ref=part,
                dst_ref=goal,
                send_sem=send.at[place, k],
                recv_sem=recv.at[place, k],
                device_id={"row": row_peers[k]},
                device_id_type=MESH,
            )
            for k in range(row_n - 1)
        ]

    def gathers(place, part):
        field, half = order[place]
        return row_copies(place, part, st.at[0, field, half, mine], row_send, row_recv)

    def at_place(place, action):
        if order[place][0] == SRC:

            @pl.when(seg == 0)
            def _():
                action(fresh_part(place))

            @pl.when(seg > 0)
            def _():
                action(plain_part(place))
        else:
            action(plain_part(place))

    def each(copies, action):
        for copy in copies:
            action(copy)

    weight_copy = pltpu.make_async_copy(weights, held_weights, weight_sem.at[0])
    weight_copy.start()
    for place in range(6):
        at_place(place, lambda part: own_copy(place, part).start())

    def late_parts(of_target):
        parts = []
        for tick in range(ticks - 1):
            for half in range(2):
                if of_target:
                    parts.append((target.at[tick, :, lanes(half)], aims.at[tick, half, mine]))
                else:
                    parts.append(
                        (fresh.at[tick + 1, :, lanes(half)], st.at[tick + 1, SRC, half, mine])
                    )
        return parts

    def late_each(action):
        for of_target, here in ((False, seg == 0), (True, seg == seg_n - 1)):

            @pl.when(here)
            def _(of_target=of_target):
                for place, (part, goal) in enumerate(late_parts(of_target)):
                    own = functools.partial(
                        pltpu.make_async_copy, part, goal, late_sem.at[place]
                    )
                    action(own, row_copies(place, part, goal, late_send, late_recv))

    always = len(row_peers) + len(dp_peers)
    pl.semaphore_wait(barrier, always + not_first.astype(jnp.int32) + not_last.astype(jnp.int32))

    for place in range(6):
        at_place(place, lambda part: each(gathers(place, part), lambda copy: copy.start()))

    def late_start(own, copies):
        own().start()
        each(copies, lambda copy: copy.start())

    def late_landed(own, copies):
        own().wait()
        each(copies, lambda copy: copy.wait_recv())

    def late_sent(own, copies):
        each(copies, lambda copy: copy.wait_send())

    def landed_at(places):
        for place in places:

            def wait(part):
                own_copy(place, part).wait()
                each(gathers(place, part), lambda copy: copy.wait_recv())

            at_place(place, wait)

    late_each(late_start)

    def store_kernel(ref, pair, tap, value):
        high, low = split_float(value)
        base = tap * (2 * chans)
        for part in range(2):
            rows = pl.ds(pl.multiple_of(base + part * chans, chans), chans)
            ref[pair, rows, :chans] = high
            ref[pair, rows, chans:] = low

    def prepare(index, carry):
        pair = index // 9
        tap = index - 9 * pair
        value = held_weights[pair, pl.ds(pl.multiple_of(tap * chans, chans), chans), :]
        store_kernel(w_fwd, pair, tap, value)
        store_kernel(w_flip, pair, 8 - tap, value.T)
        return carry

    weight_copy.wait()
    lax.fori_loop(0, 36, prepare, 0)

    rim = jnp.zeros((width, 2 * chans), jnp.bfloat16)
    for side in range(3):
        for start in (0, width + cells):
            pad_fwd[side, start : start + width] = rim
            pad_src[side, start : start + width] = rim
            for slot in range(8):
                pad_cot[slot, side, start : start + width] = rim

    column = lax.rem(lax.broadcasted_iota(jnp.int32, (cells, chans), 0), width)

    def fill(view, value):
        before = jnp.where(column == 0, 0.0, pltpu.roll(value, 1, 0))
        after = jnp.where(column == width - 1, 0.0, pltpu.roll(value, cells - 1, 0))
        for side, shifted in enumerate((before, value, after)):
            high, low = split_float(shifted)
            view[side, width : width + cells, :chans] = high
            view[side, width : width + cells, chans:] = low

    def conv(view, kernel):
        patches = jnp.concatenate(
            [
                view[tap % 3, (tap // 3) * width : (tap // 3) * width + cells, :]
                for tap in range(9)
            ],
            axis=1,
        )
        both = jnp.dot(patches, kernel, preferred_element_type=jnp.float32)
        return both[:, :chans] + both[:, chans:]

    doubled = jnp.full((cells, chans), blocks[0], jnp.int32) == 2

    def pair_of(step):
        return 2 * (1 - step // 2) + 1 - step % 2

    def slot_of(tick, step):
        return 4 * (tick % 2) + step

    def forward_step(tick, step):
        even = step % 2 == 0
        source, goal = (1, 0) if even else (0, 1)
        value = st[tick, SRC, source] if step == 0 else keep[source]
        fill(pad_fwd, jax.nn.silu(value))
        base = st[tick, SRC, goal] if step < 2 else keep[goal]
        value = base + conv(pad_fwd, w_fwd[step])
        if step >= 2:
            produced[tick, SRC, goal] = jnp.where(doubled, value, keep[goal])
        keep[goal] = value

    def backward_open(tick, step):
        even = step % 2 == 0
        holder = st if step == 0 else produced
        source = holder[tick, OUT, 0 if even else 1]
        cot = holder[tick, GRAD, 1 if even else 0]
        logistic = jax.nn.sigmoid(source)
        active = source * logistic
        fill(pad_src, active)
        fill(pad_cot.at[slot_of(tick, step)], cot)
        high, low = split_float(active.T)
        src_t[slot_of(tick, step), :chans] = high
        src_t[slot_of(tick, step), chans:] = low
        return logistic * (1.0 + source * (1.0 - logistic))

    def backward_close(tick, step, slope, send):
        even = step % 2 == 0
        out_goal, grad_goal = (1, 0) if even else (0, 1)
        holder = st if step < 2 else produced
        out_old = holder[tick, OUT, out_goal]
        grad_old = holder[tick, GRAD, grad_goal]
        rebuilt = conv(pad_src, w_fwd[pair_of(step)])
        produced[tick, OUT, out_goal] = out_old - rebuilt
        if send and step >= 2:
            seg_start(tick, OUT, out_goal)
        added = conv(pad_cot.at[slot_of(tick, step)], w_flip[pair_of(step)]) * slope
        produced[tick, GRAD, grad_goal] = grad_old + added
        if send and step >= 2:
            seg_start(tick, GRAD, grad_goal)
        if step == 1:
            for half in range(2):
                for field in (OUT, GRAD):
                    produced[tick, field, half] = jnp.where(
                        doubled, produced[tick, field, half], st[tick, field, half]
                    )

    first_tap = jnp.minimum((row * (9 * chans // row_n)) // chans, 9 - taps)

    def kernel_grads(tick, step):
        pair = pair_of(step)
        for extra in range(taps):
            other = 8 - first_tap - extra
            down = other // 3
            side = other - 3 * down
            cots = pad_cot[slot_of(tick, step), side, pl.ds(pl.multiple_of(down * width, width), cells), :]
            four = jnp.dot(src_t[slot_of(tick, step)], cots, preferred_element_type=jnp.float32)
            two = four[:chans] + four[chans:]
            value = two[:, :chans] + two[:, chans:]
            rows = slice(extra * chans, (extra + 1) * chans)
            if tick > 0:
                value = value + sums[pair, rows]
            sums[pair, rows] = value

    def seg_copy(tick, field, half):
        by = 1 if field == SRC else -1
        slot = (tick * 3 + field) * 2 + half

        def make(to):
            return pltpu.make_async_remote_copy(
                src_ref=produced.at[tick, field, half],
                dst_ref=st.at[tick + 1, field, half],
                send_sem=seg_send.at[slot],
                recv_sem=seg_recv.at[slot],
                device_id={"segment": to},
                device_id_type=MESH,
            )

        return make, by

    def seg_start(tick, field, half):
        make, by = seg_copy(tick, field, half)

        @pl.when(not_last if by > 0 else not_first)
        def _():
            make(seg + by).start()

    def seg_wait_recv(tick, field, half):
        make, by = seg_copy(tick, field, half)

        @pl.when(not_first if by > 0 else not_last)
        def _():
            make(seg - by).wait_recv()

    def seg_wait_send(tick, field, half):
        make, by = seg_copy(tick, field, half)

        @pl.when(not_last if by > 0 else not_first)
        def _():
            make(seg + by).wait_send()

    offset = row * (9 * chans // row_n) - first_tap * chans

    def chunk_rows(index):
        return pl.ds(pl.multiple_of(offset + index * chunk, 16), chunk)

    def red_places(level):
        span = 1 << (level + 1)
        count = dp_n // span
        start = sum(dp_n >> (lev + 1) for lev in range(level))
        return span, count, start

    def red_copies(pair, level):
        span, count, start = red_places(level)
        away = lax.rem(dp_peers[level], span)
        return [
            pltpu.make_async_remote_copy(
                src_ref=sums.at[pair, chunk_rows(away + span * j)],
                dst_ref=landed.at[pair, start + j],
                send_sem=red_send.at[pair, start + j],
                recv_sem=red_recv.at[pair, start + j],
                device_id={"dp": dp_peers[level]},
                device_id_type=MESH,
            )
            for j in range(count)
        ]

    def red_start(pair, level):
        if level < levels:
            for copy in red_copies(pair, level):
                copy.start()

    def red_finish(pair, level):
        span, count, start = red_places(level)
        own = lax.rem(dp, span)
        for j, copy in enumerate(red_copies(pair, level)):
            copy.wait_recv()
            rows = chunk_rows(own + span * j)
            sums[pair, rows] = sums[pair, rows] + landed[pair, start + j]

    for tick in range(ticks):
        final = tick == ticks - 1
        for step in range(4):
            if step == 0:
                if tick == 0:
                    landed_at((0, 1))
                else:
                    seg_wait_recv(tick - 1, OUT, 0)
                    seg_wait_recv(tick - 1, GRAD, 1)
            slope = backward_open(tick, step)
            if final:
                kernel_grads(tick, step)
                red_start(pair_of(step), 0)
            if step == 0:
                if tick == 0:
                    landed_at((2, 3))
                else:
                    seg_wait_recv(tick - 1, OUT, 1)
                    seg_wait_recv(tick - 1, GRAD, 0)
            backward_close(tick, step, slope, not final)
        if tick == 0:
            landed_at((4, 5))
            late_each(late_landed)
        else:
            seg_wait_recv(tick - 1, SRC, 0)
            seg_wait_recv(tick - 1, SRC, 1)
        for step in range(4):
            if final and levels > 0:
                red_finish(pair_of(step), 0)
                red_start(pair_of(step), 1)
            forward_step(tick, step)
            if not final and step >= 2:
                seg_start(tick, SRC, step % 2)
        if not final:

            @pl.when(seg == seg_n - 1)
            def _(tick=tick):
                for half in range(2):
                    value = produced[tick, SRC, half]
                    st[tick + 1, OUT, half] = value
                    st[tick + 1, GRAD, half] = value - aims[tick, half]

            for step in range(4):
                kernel_grads(tick, step)

    last = ticks - 1
    for half in range(2):
        leaving[:, lanes(half)] = produced[last, SRC, half, mine]
        for field in (OUT, GRAD):
            sent_back[field - 1, :, lanes(half)] = produced[last, field, half, mine]

    for level in range(1, levels):
        for step in range(4):
            red_finish(pair_of(step), level)
            red_start(pair_of(step), level + 1)
    twice = jnp.full((chunk, chans), blocks[0], jnp.int32) == 2
    for pair in range(4):
        total = sums[pair, chunk_rows(dp)] * scale
        if pair >= 2:
            total = jnp.where(twice, total, 0.0)
        grads_out[pair] = total

    for place in range(6):
        at_place(place, lambda part: each(gathers(place, part), lambda copy: copy.wait_send()))
    late_each(late_sent)
    for tick in range(ticks - 1):
        for field in (SRC, OUT, GRAD):
            for half in range(2):
                seg_wait_send(tick, field, half)
    for level in range(levels):
        for pair in range(4):
            for copy in red_copies(pair, level):
                copy.wait_send()


def per_device(axis_sizes, fresh, target, carried, returning, weights, section_blocks):
    seg_n, row_n, dp_n = axis_sizes
    ticks, crops, rows_here, width, both = fresh.shape
    assert crops == 1 and dp_n & (dp_n - 1) == 0
    chans = both // 2
    local = rows_here * width
    cells = local * row_n
    held = 9 * chans // row_n
    taps = max(-(-(r + 1) * held // chans) - r * held // chans for r in range(row_n))
    reach = dp_n - 1
    chunk = held // dp_n
    scale = 1.0 / math.sqrt(ticks * dp_n * cells)
    sizes = (ticks, seg_n, row_n, dp_n, width, local, chans, taps, reach, scale)
    pairs = 4
    f32, b16 = jnp.float32, jnp.bfloat16
    padded = cells + 2 * width
    dma = pltpu.SemaphoreType.DMA
    peers = max(row_n - 1, 1)
    late = 2 * max(ticks - 1, 1)
    vmem = pl.BlockSpec(memory_space=pltpu.VMEM)
    flops = ticks * 4 * (3 * 9 + taps) * 2 * cells * chans * chans * 4
    grads_out, leaving, sent_back = pl.pallas_call(
        functools.partial(kernel_body, sizes),
        out_shape=(
            jax.ShapeDtypeStruct((pairs, chunk, chans), f32),
            jax.ShapeDtypeStruct((local, both), f32),
            jax.ShapeDtypeStruct((2, local, both), f32),
        ),
        in_specs=[pl.BlockSpec(memory_space=pltpu.HBM)] * 5 + [pl.BlockSpec(memory_space=pltpu.SMEM)],
        out_specs=(vmem, vmem, vmem),
        scratch_shapes=[
            pltpu.VMEM((ticks, 3, 2, cells, chans), f32),
            pltpu.VMEM((ticks, 3, 2, cells, chans), f32),
            pltpu.VMEM((max(ticks - 1, 1), 2, cells, chans), f32),
            pltpu.VMEM((2, cells, chans), f32),
            pltpu.VMEM((pairs, 18 * chans, 2 * chans), b16),
            pltpu.VMEM((pairs, 18 * chans, 2 * chans), b16),
            pltpu.VMEM((3, padded, 2 * chans), b16),
            pltpu.VMEM((3, padded, 2 * chans), b16),
            pltpu.VMEM((8, 3, padded, 2 * chans), b16),
            pltpu.VMEM((8, 2 * chans, cells), b16),
            pltpu.VMEM((pairs, taps * chans, chans), f32),
            pltpu.VMEM((pairs, max(reach, 1), chunk, chans), f32),
            dma((6, peers)),
            dma((6, peers)),
            dma((late, peers)),
            dma((late, peers)),
            dma((6 * ticks,)),
            dma((6 * ticks,)),
            dma((pairs, max(reach, 1))),
            dma((pairs, max(reach, 1))),
            pltpu.VMEM((pairs, 9 * chans, chans), f32),
            dma((6,)),
            dma((late,)),
            dma((1,)),
        ],
        cost_estimate=pl.CostEstimate(flops=flops, bytes_accessed=1 << 22, transcendentals=1 << 20),
        compiler_params=pltpu.CompilerParams(
            collective_id=0, has_side_effects=True, vmem_limit_bytes=62 << 20
        ),
    )(
        fresh.reshape(ticks, local, both),
        target.reshape(-1, local, both),
        carried.reshape(local, both),
        returning.reshape(2, local, both),
        weights.reshape(pairs, 9 * chans, chans),
        section_blocks,
    )
    return (
        grads_out.reshape(1, 2, 2, chunk, chans),
        leaving.reshape(1, 1, rows_here, width, both),
        sent_back.reshape(1, 2, 1, rows_here, width, both),
    )


def solution(mesh):
    axis_sizes = (mesh.shape["segment"], mesh.shape["row"], mesh.shape["dp"])
    return jax.shard_map(
        functools.partial(per_device, axis_sizes),
        mesh=mesh,
        in_specs=(
            P(None, "dp", "row", None, None),
            P(None, "dp", "row", None, None),
            P("segment", "dp", "row", None, None),
            P("segment", None, "dp", "row", None, None),
            P("segment", None, None, None, None),
            P("segment"),
        ),
        out_specs=(
            P("segment", None, None, ("row", "dp"), None),
            P("segment", "dp", "row", None, None),
            P("segment", None, "dp", "row", None, None),
        ),
        check_vma=False,
    )
```
